512 devices in a mesh: gx: 8 (over z), gy: 8 (over y_hi, core), gz: 8 (over y_lo, x).
Axes of the slice: x: 4, y: 8 (y_hi: 4, y_lo: 2; y = y_hi * 2 + y_lo), z: 8, core: 2. Of those that a mesh axis runs over, the one named last changes fastest.
Arguments:
- source_coefs: float32 [2, 5, 5, 5, 1048576], P(None, None, None, None, ('gx', 'gy', 'gz')), may hold values from -6 to 6
- speed_first: float32 [16, 16, 16], replicated, may hold values from 0.5 to 2
- speed_second: float32 [16, 32, 16], replicated, may hold values from 0.5 to 2
Outputs:
- image_coefs: float32 [2, 5, 5, 5, 1048576], P(None, None, None, None, ('gx', 'gy', 'gz'))
The draws below stay inside these ranges and needn't reach their ends.
All inputs are finite; a program needn't handle non-finite values.
Results may differ from the reference program's by a relative error of at most 0.00045.
Values sent between devices are 32-bit elements; how exact they have to be, the bound alone decides.
No kernel may reach another device: no remote copies, remote signals or barrier semaphores. Data moves between devices by JAX's collectives and lax.ppermute only.
A program may use at most 64 MiB of HBM per device.

```python
import math
import jax
import jax.numpy as jnp
import numpy as np
from jax import lax

CHEB = 5
KMAX = 512
TX = 8
TY = 16
TZ = 16
TBOX = 2048
ALLBOX = 1048576
N_GX = 8
N_GY = 8
N_GZ = 8


def shard_levels(stream_key, dims, cuts, low, top_value):
    level = 1.0
    for dim, blocks in cuts:
        heights = jax.random.uniform(jax.random.fold_in(jax.random.fold_in(stream_key, 6), dim), (blocks,), jnp.float32, low / len(cuts), top_value / len(cuts))
        level = level * jnp.repeat(jnp.exp(heights), dims[dim] // blocks).reshape((-1,) + (1,) * (len(dims) - 1 - dim))
    return level


def gaussian(own_key, shape, deviation, bound, shards=(), kind=jnp.bfloat16):
    values = deviation * jax.random.normal(own_key, shape, jnp.float32)
    if shards:
        values = values * shard_levels(own_key, shape, shards, -0.22, 0.18)
    return jnp.clip(values, -bound, bound).astype(kind)


def setup_inputs(seed: int = 0) -> dict:
    seeds = jax.random.split(jax.random.key(seed), 4)
    source_coefs = gaussian(seeds[0], (2, CHEB, CHEB, CHEB, ALLBOX), 1.0, 6.0, ((4, 512),), jnp.float32)
    speed_first = jnp.clip(jnp.exp(jax.random.uniform(seeds[1], (2 * TX, TY, TZ), jnp.float32, math.log(0.5), math.log(2.0))), 0.5, 2.0)
    speed_second = jnp.clip(jnp.exp(jax.random.uniform(seeds[2], (2 * TX, 2 * TY, TZ), jnp.float32, math.log(0.5), math.log(2.0))), 0.5, 2.0)
    return {"source_coefs": source_coefs, "speed_first": speed_first, "speed_second": speed_second}


TWO_PI = 2.0 * math.pi

def chebyshev_points():
    return 0.5 * np.cos(np.pi * np.arange(CHEB) / (CHEB - 1))

def lagrange_tables():
    chebyshev = chebyshev_points()
    tables = np.ones((2, CHEB, CHEB))
    for child_side in range(2):
        shifted = (chebyshev + child_side - 0.5) / 2.0
        for target in range(CHEB):
            for factor in range(CHEB):
                if factor != target:
                    tables[child_side, target, :] *= (shifted - chebyshev[factor]) / (chebyshev[target] - chebyshev[factor])
    return jnp.asarray(tables, jnp.float32)

def phase_cycles(targets, speeds, grids, center):
    target_x, target_y, target_z = targets
    grid_x, grid_y, grid_z = grids
    delta_x = grid_x - center[0]
    delta_y = grid_y - center[1]
    delta_z = grid_z - center[2]
    along_target = delta_x[:, None, None, None] * target_x + delta_y[None, :, None, None] * target_y + delta_z[None, None, :, None] * target_z
    numerator = (delta_x * (grid_x + center[0]))[:, None, None] + (delta_y * (grid_y + center[1]))[None, :, None] + (delta_z * (grid_z + center[2]))[None, None, :]
    radius = jnp.sqrt((grid_x * grid_x)[:, None, None] + (grid_y * grid_y)[None, :, None] + (grid_z * grid_z)[None, None, :])
    radius = radius + jnp.sqrt(center[0] * center[0] + center[1] * center[1] + center[2] * center[2])
    return along_target + speeds * (numerator / radius)[..., None]

def box_grids(center, widths, merge_dim, child_side):
    chebyshev = jnp.asarray(chebyshev_points(), jnp.float32)
    grids = [center[dim_index] + widths[dim_index] * chebyshev for dim_index in range(3)]
    if merge_dim >= 0:
        offset = child_side.astype(jnp.float32) - 0.5
        grids[merge_dim] = center[merge_dim] + widths[merge_dim] * (chebyshev + offset) * 0.5
    return grids

def child_term(stacked, child_side, merge_dim, targets, speeds, center, widths):
    grids = box_grids(center, widths, merge_dim, child_side)
    angle = TWO_PI * phase_cycles(targets, speeds, grids, center)
    cosine = jnp.cos(angle)
    sine = jnp.sin(angle)
    turned = jnp.stack([stacked[0] * cosine + stacked[1] * sine, stacked[1] * cosine - stacked[0] * sine])
    tables = lagrange_tables()
    table = jnp.where(child_side == 0, tables[0], tables[1])
    if merge_dim == 0:
        return jnp.einsum('pm,cmqrn->cpqrn', table, turned, precision=lax.Precision.HIGHEST)
    return jnp.einsum('qm,cpmrn->cpqrn', table, turned, precision=lax.Precision.HIGHEST)

def finish(total, targets, speeds, center, widths):
    grids = box_grids(center, widths, -1, None)
    angle = TWO_PI * phase_cycles(targets, speeds, grids, center)
    cosine = jnp.cos(angle)
    sine = jnp.sin(angle)
    return jnp.stack([total[0] * cosine - total[1] * sine, total[0] * sine + total[1] * cosine])

def target_boxes(count, first_side, second_side):
    box_order = jnp.arange(count, dtype=jnp.int32)
    along_x = box_order // (TY * TZ)
    along_y = box_order // TZ % TY
    along_z = box_order % TZ
    target_x = ((2 * along_x + first_side).astype(jnp.float32) + 0.5) / (2.0 * TX)
    if second_side is None:
        target_y = (along_y.astype(jnp.float32) + 0.5) / TY
    else:
        target_y = ((2 * along_y + second_side).astype(jnp.float32) + 0.5) / (2.0 * TY)
    target_z = (along_z.astype(jnp.float32) + 0.5) / TZ
    return (target_x, target_y, target_z)

def first_speeds(speed_first, first_side):
    shaped = speed_first.reshape(TX, 2, TY, TZ)
    return lax.dynamic_index_in_dim(shaped, first_side, 1, keepdims=False).reshape(-1)

def second_speeds(speed_second, first_side, second_side):
    shaped = speed_second.reshape(TX, 2, TY, 2, TZ)
    picked = lax.dynamic_index_in_dim(shaped, first_side, 1, keepdims=False)
    return lax.dynamic_index_in_dim(picked, second_side, 2, keepdims=False).reshape(-1)

def reference(source_coefs, speed_first, speed_second):
    count = TBOX
    devices = N_GX * N_GY * N_GZ
    by_device = jnp.moveaxis(source_coefs.reshape(2, CHEB, CHEB, CHEB, devices, count), 4, 0)
    width_x = KMAX // N_GX
    width_y = KMAX // N_GY
    width_z = KMAX // N_GZ
    half_x = N_GX // 2
    half_y = N_GY // 2

    def locate(device):
        index_x = device // (N_GY * N_GZ)
        index_y = device // N_GZ % N_GY
        index_z = device % N_GZ
        return (index_x, index_y, index_z)

    def first_level(device):
        index_x, index_y, index_z = locate(device)
        side_x = index_x // half_x
        box_y = 2 * (index_y % half_y) + index_y // half_y
        partner = device + (1 - 2 * side_x) * (half_x * N_GY * N_GZ)
        center_one = (((2 * (index_x % half_x) + 1) * width_x).astype(jnp.float32), (box_y.astype(jnp.float32) + 0.5) * width_y, (index_z.astype(jnp.float32) + 0.5) * width_z)
        widths_one = (2.0 * width_x, 1.0 * width_y, 1.0 * width_z)
        targets = target_boxes(count, side_x, None)
        speeds = first_speeds(speed_first, side_x)
        total = child_term(by_device[device], side_x, 0, targets, speeds, center_one, widths_one) + child_term(by_device[partner], 1 - side_x, 0, targets, speeds, center_one, widths_one)
        return finish(total, targets, speeds, center_one, widths_one)
    level_one = lax.map(first_level, jnp.arange(devices, dtype=jnp.int32))

    def second_level(device):
        index_x, index_y, index_z = locate(device)
        side_x = index_x // half_x
        side_y = index_y // half_y
        partner = device + (1 - 2 * side_y) * (half_y * N_GZ)
        center_two = (((2 * (index_x % half_x) + 1) * width_x).astype(jnp.float32), ((2 * (index_y % half_y) + 1) * width_y).astype(jnp.float32), (index_z.astype(jnp.float32) + 0.5) * width_z)
        widths_two = (2.0 * width_x, 2.0 * width_y, 1.0 * width_z)
        targets = target_boxes(count, side_x, side_y)
        speeds = second_speeds(speed_second, side_x, side_y)
        total = child_term(level_one[device], side_y, 1, targets, speeds, center_two, widths_two) + child_term(level_one[partner], 1 - side_y, 1, targets, speeds, center_two, widths_two)
        return finish(total, targets, speeds, center_two, widths_two)
    result = lax.map(second_level, jnp.arange(devices, dtype=jnp.int32))
    return jnp.moveaxis(result, 0, 4).reshape(2, CHEB, CHEB, CHEB, devices * count)
```

```python
import functools

import jax
import jax.numpy as jnp
import numpy as np
from jax import lax
from jax.experimental import pallas as pl
from jax.experimental.pallas import tpu as pltpu
from jax.sharding import PartitionSpec as P

CHEB = 5
KMAX = 512
TX = 8
TY = 16
TZ = 16
ROWS = 8
LANES = 128
AXES = ("gx", "gy", "gz")
PIECES = ((0, 3), (3, 2))
ROUNDER = 1.5 * 2.0**23
SINE = (4.442867903031852, -7.307443421308049, 3.594788078718595, -0.784374031470659)
COSINE = (
    1.41421349656502,
    -6.978850988239763,
    5.739461170697818,
    -1.8835629874053614,
    0.3106981920186687,
)

POINTS = 0.5 * np.cos(np.pi * np.arange(CHEB) / (CHEB - 1))
POINTS[CHEB // 2] = 0.0


def lagrange_table():
    shifted = (POINTS - 0.5) / 2.0
    table = np.ones((CHEB, CHEB))
    for target in range(CHEB):
        for factor in range(CHEB):
            if factor != target:
                table[target] *= (shifted - POINTS[factor]) / (POINTS[target] - POINTS[factor])
    return table


TABLE = lagrange_table()


def from_partner(value, stride):
    mask = 2**stride
    pairs = [(source, source ^ mask) for source in range(lax.axis_size(AXES))]
    return lax.ppermute(value, AXES, pairs)


def fraction(cycles):
    return cycles - ((cycles + ROUNDER) - ROUNDER)


def turn(cycles):
    part = fraction(cycles)
    square = part * part
    sine = SINE[-1] * square + SINE[-2]
    for factor in SINE[-3::-1]:
        sine = sine * square + factor
    sine = sine * part
    cosine = COSINE[-1] * square + COSINE[-2]
    for factor in COSINE[-3::-1]:
        cosine = cosine * square + factor
    return 1.0 - sine * sine, sine * cosine


def forward(value, cycles):
    cosine, sine = turn(cycles)
    return value[0] * cosine - value[1] * sine, value[0] * sine + value[1] * cosine


def backward(value, cycles):
    cosine, sine = turn(cycles)
    return value[0] * cosine + value[1] * sine, value[1] * cosine - value[0] * sine


def merge(values):
    merged = []
    for target in range(CHEB):
        parts = []
        for part in range(2):
            total = float(TABLE[target, 1]) * values[1][part]
            for point in (2, 3):
                total = total + float(TABLE[target, point]) * values[point][part]
            if target == 2:
                total = total + values[0][part]
            if target == 4:
                total = total + values[4][part]
            parts.append(total)
        merged.append(tuple(parts))
    return merged


def flipped(first, second):
    return [
        (a[0] + b[0], a[1] + b[1]) for a, b in zip(first, second[::-1], strict=True)
    ]


class Targets:
    def __init__(self, half, table, sides, speeds):
        row = lax.broadcasted_iota(jnp.int32, (ROWS, LANES), 0) + ROWS * half
        lane = lax.broadcasted_iota(jnp.int32, (ROWS, LANES), 1)
        self.along_x = lax.shift_right_logical(row, 1).astype(jnp.float32)
        self.along_y = (
            lax.bitwise_and(row, 1) * 8 + lax.shift_right_logical(lane, 4)
        ).astype(jnp.float32)
        self.along_z = lax.bitwise_and(lane, 15).astype(jnp.float32)
        self.z = (self.along_z + 0.5) / TZ
        self.y = (self.along_y + 0.5) / TY
        self.table = table
        self.side_x, self.side_y = sides[0], sides[1]
        self.sign_x = 1.0 - 2.0 * self.side_x.astype(jnp.float32)
        self.sign_y = 1.0 - 2.0 * self.side_y.astype(jnp.float32)
        self.speeds = [speeds[k, ROWS * half : ROWS * (half + 1), :] for k in range(5)]

    def x(self, far):
        side = self.side_x.astype(jnp.float32)
        side = 1.0 - side if far else side
        return (2.0 * self.along_x + side + 0.5) / (2.0 * TX)

    def fine_y(self, far):
        side = self.side_y.astype(jnp.float32)
        side = 1.0 - side if far else side
        return (2.0 * self.along_y + side + 0.5) / (2.0 * TY)

    def point(self, index):
        return self.table[8, index]

    def radius(self, which, p, q, r):
        return self.table[which, p * (CHEB * CHEB) + q * CHEB + r]


def end(side, index):
    return index + side * (CHEB - 1 - 2 * index)


def first_merge(at, weights, which, sign_x, sign_y, flips, x, speed, q, r, r_local):
    flip_x, flip_y = flips
    rows = at.point(q) * (64.0 * sign_y) * at.y + at.point(r) * 64.0 * at.z
    rows = fraction(rows)
    turned = []
    for m in range(CHEB):
        cycles = (x[m] + rows) + speed * at.radius(which, m, q, r)
        point = (end(flip_x, m), end(flip_y, q), r_local)
        value = (
            weights[(*point, pl.ds(0, ROWS, stride=2), slice(None))],
            weights[(*point, pl.ds(1, ROWS, stride=2), slice(None))],
        )
        turned.append(backward(value, cycles))
    return merge(turned)


def first_x(sign, x):
    return [fraction((sign * (64.0 * float(z - 0.5))) * x) for z in POINTS]


def between_y(at, sign, fine):
    return [
        fraction(sign * (float(64.0 * z) * at.y - float(64.0 * (z - 0.5)) * fine)) for z in POINTS
    ]


def second_merge(at, level, tables, between, speeds, p, r, r_local):
    turned = []
    for q in range(CHEB):
        cycles = (
            between[q]
            + speeds[0] * at.radius(tables[0], p, q, r)
            - speeds[1] * at.radius(tables[1], p, q, r)
        )
        turned.append(forward((level[p, q, r_local, 0], level[p, q, r_local, 1]), cycles))
    return merge(turned)


def put(ref, values, *place):
    ref[(*place, 0)] = values[0]
    ref[(*place, 1)] = values[1]


def level_kernel(first, count, table, sides, speeds, own, got, level, send):
    at = Targets(0, table, sides, speeds)
    x = at.x(False)
    x_own, x_got = first_x(at.sign_x, x), first_x(-at.sign_x, x)

    def one_level(q, carry):
        for k in range(count):
            mine = first_merge(
                at, own, 0, at.sign_x, at.sign_y, (at.side_x, at.side_y), x_own, at.speeds[0], q, first + k, k
            )
            theirs = first_merge(
                at, got, 1, -at.sign_x, at.sign_y, (1 - at.side_x, at.side_y), x_got, at.speeds[0], q, first + k, k
            )
            for p, value in enumerate(flipped(mine, theirs)):
                put(level, value, p, q, k)
        return carry

    lax.fori_loop(0, CHEB, one_level, 0)
    between = between_y(at, at.sign_y, at.fine_y(True))

    def two_level(p, carry):
        for k in range(count):
            shares = second_merge(
                at, level, (3, 5), between, (at.speeds[0], at.speeds[3]), p, first + k, k
            )
            for q, value in enumerate(shares):
                put(send, value, p, q, k)
        return carry

    lax.fori_loop(0, CHEB, two_level, 0)


def both_kernel(first, count, far, table, sides, speeds, own, got, send, level_own, level_got):
    at = Targets(1, table, sides, speeds)
    x = first_x(at.sign_x, at.x(far))
    speed, speed_two = at.speeds[int(far)], at.speeds[4 if far else 2]

    def one_level(q, carry):
        for k in range(count):
            for weights, which, sign_y, flip_y, level in (
                (own, 0, at.sign_y, at.side_y, level_own),
                (got, 2, -at.sign_y, 1 - at.side_y, level_got),
            ):
                merged = first_merge(
                    at, weights, which, at.sign_x, sign_y, (at.side_x, flip_y), x, speed, q, first + k, k
                )
                for p, value in enumerate(merged):
                    put(level, value, p, q, k)
        return carry

    lax.fori_loop(0, CHEB, one_level, 0)
    fine = at.fine_y(False)
    between_own, between_got = between_y(at, at.sign_y, fine), between_y(at, -at.sign_y, fine)

    def two_level(p, carry):
        for k in range(count):
            mine = second_merge(at, level_own, (3, 5), between_own, (speed, speed_two), p, first + k, k)
            theirs = second_merge(at, level_got, (4, 6), between_got, (speed, speed_two), p, first + k, k)
            for q, value in enumerate(flipped(mine, theirs)):
                put(send, value, p, q, k)
        return carry

    lax.fori_loop(0, CHEB, two_level, 0)


def last_kernel(half, first, table, sides, speeds, level, got, *rest):
    out = rest[-1]
    at = Targets(half, table, sides, speeds)
    r = first + pl.program_id(0)
    x, fine = at.x(False), at.fine_y(False)
    along_y = [fraction((at.sign_y * float(128.0 * z)) * fine) for z in POINTS]
    along_z = fraction(at.point(r) * 64.0 * at.z)
    along_yz = [value + along_z for value in along_y]
    between = between_y(at, at.sign_y, fine)

    def one_p(p, carry):
        along_x = fraction((at.sign_x * 128.0 * at.point(p)) * x)
        if half == 0:
            mine = second_merge(
                at, level, (3, 5), between, (at.speeds[0], at.speeds[2]), p, r, 0
            )
        for q in range(CHEB):
            if half == 0:
                value = mine[q]
                other = (got[p, CHEB - 1 - q, 0, 0], got[p, CHEB - 1 - q, 0, 1])
            else:
                value = (level[p, q, 0, 0], level[p, q, 0, 1])
                other = (got[CHEB - 1 - p, q, 0, 0], got[CHEB - 1 - p, q, 0, 1])
            cycles = (along_x + along_yz[q]) + at.speeds[2] * at.radius(7, p, q, r)
            value = forward((value[0] + other[0], value[1] + other[1]), cycles)
            point = (end(at.side_x, p), end(at.side_y, q), 0)
            out[(*point, pl.ds(0, ROWS, stride=2), slice(None))] = value[0]
            out[(*point, pl.ds(1, ROWS, stride=2), slice(None))] = value[1]
        return carry

    lax.fori_loop(0, CHEB, one_p, 0)


SMEM = pl.BlockSpec(memory_space=pltpu.SMEM)
VMEM = pl.BlockSpec(memory_space=pltpu.VMEM)


def complex_shape(count):
    return (CHEB, CHEB, count, 2, ROWS, LANES)


def cost(sets):
    return pl.CostEstimate(flops=sets * ROWS * LANES * 60, bytes_accessed=sets * 20000, transcendentals=0)


def run_level(first, count, facts, own, got):
    shape = jax.ShapeDtypeStruct(complex_shape(count), jnp.float32)
    return pl.pallas_call(
        functools.partial(level_kernel, first, count),
        in_specs=[SMEM, SMEM, VMEM, VMEM, VMEM],
        out_specs=[VMEM, VMEM],
        out_shape=[shape, shape],
        cost_estimate=cost(75 * count),
        name=f"level_{first}",
    )(*facts, own, got)


def run_both(first, count, far, facts, own, got):
    return pl.pallas_call(
        functools.partial(both_kernel, first, count, far),
        in_specs=[SMEM, SMEM, VMEM, VMEM, VMEM],
        out_specs=VMEM,
        out_shape=jax.ShapeDtypeStruct(complex_shape(count), jnp.float32),
        scratch_shapes=[pltpu.VMEM(complex_shape(count), jnp.float32)] * 2,
        cost_estimate=cost(100 * count),
        name=f"both_{first}_{int(far)}",
    )(*facts, own, got)


def run_last(half, first, count, facts, level, got, out):
    block = (CHEB, CHEB, 1, 2, ROWS, LANES)
    in_specs = [SMEM, SMEM, VMEM] + [pl.BlockSpec(block, lambda i: (0, 0, i, 0, 0, 0))] * 2
    operands = [*facts, level, got]
    aliases = {}
    if out is not None:
        in_specs.append(pl.BlockSpec(memory_space=pl.ANY))
        operands.append(out)
        aliases = {5: 0}
    return pl.pallas_call(
        functools.partial(last_kernel, half, first),
        grid=(count,),
        in_specs=in_specs,
        out_specs=pl.BlockSpec(
            (CHEB, CHEB, 1, 2 * ROWS, LANES), lambda i: (0, 0, first + i, half, 0)
        ),
        out_shape=jax.ShapeDtypeStruct((CHEB, CHEB, CHEB, 4 * ROWS, LANES), jnp.float32),
        input_output_aliases=aliases,
        cost_estimate=cost(50 * count),
        name=f"last_{half}_{first}",
    )(*operands)


def device_facts(speed_first, speed_second):
    width = [KMAX // lax.axis_size(axis) for axis in AXES]
    half_x, half_y = lax.axis_size("gx") // 2, lax.axis_size("gy") // 2
    index_x, index_y, index_z = (lax.axis_index(axis) for axis in AXES)
    side_x, side_y = index_x // half_x, index_y // half_y
    sign_x = 1.0 - 2.0 * side_x.astype(jnp.float32)
    sign_y = 1.0 - 2.0 * side_y.astype(jnp.float32)
    box_y = (2 * (index_y % half_y)).astype(jnp.float32) * width[1]
    center_x = ((2 * (index_x % half_x) + 1) * width[0]).astype(jnp.float32)
    center_z = (index_z.astype(jnp.float32) + 0.5) * width[2]
    own_y = box_y + (side_y.astype(jnp.float32) + 0.5) * width[1]
    far_y = box_y + (1.5 - side_y.astype(jnp.float32)) * width[1]
    middle_y = box_y + width[1]

    index = np.arange(LANES)
    inside = index < CHEB**3
    points = [
        np.where(inside, POINTS[index // step % CHEB], 0.0).astype(np.float32)
        for step in (CHEB * CHEB, CHEB, 1)
    ]
    child_x = sign_x * (width[0] * (points[0] - np.float32(0.5)))
    parent_x = sign_x * (2.0 * width[0] * points[0])
    child_y = sign_y * (width[1] * points[1])
    parent_y = sign_y * (2.0 * width[1] * points[1])
    pairs = (
        (child_x, own_y, child_y, own_y),
        (-child_x, own_y, child_y, own_y),
        (child_x, far_y, -child_y, far_y),
        (parent_x, own_y, child_y, own_y),
        (parent_x, far_y, -child_y, far_y),
        (parent_x, own_y, child_y, middle_y),
        (parent_x, far_y, -child_y, middle_y),
        (parent_x, middle_y, parent_y, middle_y),
    )
    grid_x = center_x + jnp.stack([pair[0] for pair in pairs])
    grid_y = jnp.stack([pair[1] + pair[2] for pair in pairs])
    center_y = jnp.stack([pair[3] for pair in pairs])[:, None]
    offset_z = (width[2] * points[2])[None]
    grid_z = center_z + offset_z
    numerator = (
        (grid_x - center_x) * (grid_x + center_x)
        + (grid_y - center_y) * (grid_y + center_y)
        + offset_z * (grid_z + center_z)
    )
    radius = jnp.sqrt(grid_x * grid_x + grid_y * grid_y + grid_z * grid_z) + jnp.sqrt(
        center_x * center_x + center_y * center_y + center_z * center_z
    )
    last = np.zeros((8, LANES), np.float32)
    last[0, :CHEB] = POINTS
    table = jnp.concatenate([numerator / radius, last], 0)
    sides = jnp.stack([side_x, side_y]).astype(jnp.int32)

    first = speed_first.reshape(TX, 2, TY * TZ)
    first_own = jnp.where(side_x == 0, first[:, 0], first[:, 1])
    first_far = jnp.where(side_x == 0, first[:, 1], first[:, 0])
    second = speed_second.reshape(TX, 2, TY, 2, TZ)
    second_own = jnp.where(side_x == 0, second[:, 0], second[:, 1])
    second_far = jnp.where(side_x == 0, second[:, 1], second[:, 0])
    speeds = [
        first_own,
        first_far,
        jnp.where(side_y == 0, second_own[:, :, 0], second_own[:, :, 1]),
        jnp.where(side_y == 0, second_own[:, :, 1], second_own[:, :, 0]),
        jnp.where(side_y == 0, second_far[:, :, 0], second_far[:, :, 1]),
    ]
    return table, sides, jnp.stack([speed.reshape(2 * ROWS, LANES) for speed in speeds])


def shards(source_coefs, speed_first, speed_second):
    bit_first = (lax.axis_size("gx") * lax.axis_size("gy") * lax.axis_size("gz")).bit_length() - 2
    bit_second = (lax.axis_size("gy") * lax.axis_size("gz")).bit_length() - 2
    weights = source_coefs.reshape(2, CHEB, CHEB, CHEB, 2 * ROWS, LANES)
    weights = weights.transpose(1, 2, 3, 4, 0, 5).reshape(CHEB, CHEB, CHEB, 4 * ROWS, LANES)
    raw = [
        [weights[:, :, first : first + count, 16 * half : 16 * (half + 1)] for first, count in PIECES]
        for half in range(2)
    ]
    got = [[], []]
    for k in range(len(PIECES)):
        got[0].append(from_partner(raw[0][k], bit_first))
        got[1].append(from_partner(raw[1][k], bit_second))
    facts = device_facts(speed_first, speed_second)
    levels, shares, arrived, arrived_two = [], [], [], []
    for k, (first, count) in enumerate(PIECES):
        level, send = run_level(first, count, facts, raw[0][k], got[0][k])
        levels.append(level)
        arrived.append(from_partner(send, bit_second))
        send = run_both(first, count, True, facts, raw[1][k], got[1][k])
        arrived_two.append(from_partner(send, bit_first))
        shares.append(run_both(first, count, False, facts, raw[1][k], got[1][k]))
    out = None
    for k, (first, count) in enumerate(PIECES):
        out = run_last(0, first, count, facts, levels[k], arrived[k], out)
        out = run_last(1, first, count, facts, shares[k], arrived_two[k], out)
    out = out.reshape(CHEB, CHEB, CHEB, 2 * ROWS, 2, LANES).transpose(4, 0, 1, 2, 3, 5)
    return out.reshape(source_coefs.shape)


def solution(mesh):
    in_specs = (P(None, None, None, None, ("gx", "gy", "gz")), P(), P())
    out_specs = P(None, None, None, None, ("gx", "gy", "gz"))
    return jax.shard_map(shards, mesh=mesh, in_specs=in_specs, out_specs=out_specs, check_vma=False)
```

```python
import functools

import jax
import jax.numpy as jnp
import numpy as np
from jax import lax
from jax.experimental import pallas as pl
from jax.experimental.pallas import tpu as pltpu
from jax.sharding import PartitionSpec as P

CHEB = 5
KMAX = 512
TX = 8
TY = 16
TZ = 16
ROWS = 8
LANES = 128
AXES = ("gx", "gy", "gz")
PIECES = ((0, 2), (2, 1), (3, 1), (4, 1))
HOLD = 0
GROUPS = ((0, 3), (3, 4))
VMEM_BYTES = 16 * 2**20
ROUNDER = 1.5 * 2.0**23
SINE = (4.442867903031852, -7.307443421308049, 3.594788078718595, -0.784374031470659)
COSINE = (
    1.41421349656502,
    -6.978850988239763,
    5.739461170697818,
    -1.8835629874053614,
    0.3106981920186687,
)

POINTS = 0.5 * np.cos(np.pi * np.arange(CHEB) / (CHEB - 1))
POINTS[CHEB // 2] = 0.0


def lagrange_table():
    shifted = (POINTS - 0.5) / 2.0
    table = np.ones((CHEB, CHEB))
    for target in range(CHEB):
        for factor in range(CHEB):
            if factor != target:
                table[target] *= (shifted - POINTS[factor]) / (POINTS[target] - POINTS[factor])
    return table


TABLE = lagrange_table()


def kind_of(index_x, index_y, index_z, half_x, half_y):
    return index_x % half_x ^ index_y % half_y ^ index_z


def parity(bits):
    return (bits ^ bits >> 1 ^ bits >> 2) & 1


def exchange(value, second):
    size_x, size_y, size_z = (lax.axis_size(axis) for axis in AXES)
    pairs = []
    for device in range(size_x * size_y * size_z):
        x, y, z = device // (size_y * size_z), device // size_z % size_y, device % size_z
        kind = parity(kind_of(x, y, z, size_x // 2, size_y // 2))
        if kind == int(second):
            x = (x + size_x // 2) % size_x
        else:
            y = (y + size_y // 2) % size_y
        pairs.append((device, (x * size_y + y) * size_z + z))
    return lax.ppermute(value, AXES, pairs)


def fraction(cycles):
    return cycles - ((cycles + ROUNDER) - ROUNDER)


def turn(cycles):
    part = fraction(cycles)
    square = part * part
    sine = SINE[-1] * square + SINE[-2]
    for factor in SINE[-3::-1]:
        sine = sine * square + factor
    sine = sine * part
    cosine = COSINE[-1] * square + COSINE[-2]
    for factor in COSINE[-3::-1]:
        cosine = cosine * square + factor
    return 1.0 - sine * sine, sine * cosine


def forward(value, cycles):
    cosine, sine = turn(cycles)
    return value[0] * cosine - value[1] * sine, value[0] * sine + value[1] * cosine


def backward(value, cycles):
    cosine, sine = turn(cycles)
    return value[0] * cosine + value[1] * sine, value[1] * cosine - value[0] * sine


def merge(values):
    merged = []
    for target in range(CHEB):
        parts = []
        for part in range(2):
            total = float(TABLE[target, 1]) * values[1][part]
            for point in (2, 3):
                total = total + float(TABLE[target, point]) * values[point][part]
            if target == 2:
                total = total + values[0][part]
            if target == 4:
                total = total + values[4][part]
            parts.append(total)
        merged.append(tuple(parts))
    return merged


def flipped(first, second):
    return [
        (a[0] + b[0], a[1] + b[1]) for a, b in zip(first, second[::-1], strict=True)
    ]


class Targets:
    def __init__(self, half, table, sides, speeds):
        row = lax.broadcasted_iota(jnp.int32, (ROWS, LANES), 0) + ROWS * half
        lane = lax.broadcasted_iota(jnp.int32, (ROWS, LANES), 1)
        self.along_x = lax.shift_right_logical(row, 1).astype(jnp.float32)
        self.along_y = (
            lax.bitwise_and(row, 1) * 8 + lax.shift_right_logical(lane, 4)
        ).astype(jnp.float32)
        self.along_z = lax.bitwise_and(lane, 15).astype(jnp.float32)
        self.z = (self.along_z + 0.5) / TZ
        self.y = (self.along_y + 0.5) / TY
        self.table = table
        self.half = half
        self.side_x, self.side_y = sides[0], sides[1]
        self.sign_x = 1.0 - 2.0 * self.side_x.astype(jnp.float32)
        self.sign_y = 1.0 - 2.0 * self.side_y.astype(jnp.float32)
        self.speeds = [speeds[k, ROWS * half : ROWS * (half + 1), :] for k in range(5)]

    def x(self, far):
        side = self.side_x.astype(jnp.float32)
        side = 1.0 - side if far else side
        return (2.0 * self.along_x + side + 0.5) / (2.0 * TX)

    def fine_y(self, far):
        side = self.side_y.astype(jnp.float32)
        side = 1.0 - side if far else side
        return (2.0 * self.along_y + side + 0.5) / (2.0 * TY)

    def point(self, index):
        return self.table[8, index]

    def radius(self, which, p, q, r):
        return self.table[which, p * (CHEB * CHEB) + q * CHEB + r]


def end(side, index):
    return index + side * (CHEB - 1 - 2 * index)


def first_merge(at, weights, which, sign_x, sign_y, flips, x, speed, q, r, r_local):
    flip_x, flip_y = flips
    rows = at.point(q) * (64.0 * sign_y) * at.y + at.point(r) * 64.0 * at.z
    rows = fraction(rows)
    turned = []
    for m in range(CHEB):
        cycles = (x[m] + rows) + speed * at.radius(which, m, q, r)
        point = (end(flip_x, m), end(flip_y, q), r_local)
        value = (
            weights[(*point, pl.ds(2 * ROWS * at.half, ROWS, stride=2), slice(None))],
            weights[(*point, pl.ds(2 * ROWS * at.half + 1, ROWS, stride=2), slice(None))],
        )
        turned.append(backward(value, cycles))
    return merge(turned)


def first_x(sign, x):
    return [fraction((sign * (64.0 * float(z - 0.5))) * x) for z in POINTS]


def between_y(at, sign, fine):
    return [
        fraction(sign * (float(64.0 * z) * at.y - float(64.0 * (z - 0.5)) * fine)) for z in POINTS
    ]


def second_merge(at, level, tables, between, speeds, p, r, r_local):
    turned = []
    for q in range(CHEB):
        cycles = (
            between[q]
            + speeds[0] * at.radius(tables[0], p, q, r)
            - speeds[1] * at.radius(tables[1], p, q, r)
        )
        value = (level[p, q, r_local, at.half, 0], level[p, q, r_local, at.half, 1])
        turned.append(forward(value, cycles))
    return merge(turned)


def put(ref, values, *place):
    ref[(*place, 0)] = values[0]
    ref[(*place, 1)] = values[1]


def parent(at, first, count, own, got, level):
    x = at.x(False)
    x_own, x_got = first_x(at.sign_x, x), first_x(-at.sign_x, x)

    def one(q, carry):
        for k in range(count):
            mine = first_merge(
                at, own, 0, at.sign_x, at.sign_y, (at.side_x, at.side_y), x_own, at.speeds[0], q, first + k, k
            )
            theirs = first_merge(
                at, got, 1, -at.sign_x, at.sign_y, (1 - at.side_x, at.side_y), x_got, at.speeds[0], q, first + k, k
            )
            for p, value in enumerate(flipped(mine, theirs)):
                put(level, value, p, q, k, at.half)
        return carry

    lax.fori_loop(0, CHEB, one, 0)


def share_kind_0(at, first, count, far, level, use):
    between = between_y(at, at.sign_y, at.fine_y(far))
    speeds = (at.speeds[0], at.speeds[3 if far else 2])

    def one(p, carry):
        for k in range(count):
            use(second_merge(at, level, (3, 5), between, speeds, p, first + k, k), p, k)
        return carry

    lax.fori_loop(0, CHEB, one, 0)


def share_kind_1(at, first, count, far, own, got, level_own, level_got, use):
    x = first_x(at.sign_x, at.x(far))
    speed, speed_two = at.speeds[int(far)], at.speeds[4 if far else 2]

    def one_level(q, carry):
        for k in range(count):
            for weights, which, sign_y, flip_y, level in (
                (own, 0, at.sign_y, at.side_y, level_own),
                (got, 2, -at.sign_y, 1 - at.side_y, level_got),
            ):
                merged = first_merge(
                    at, weights, which, at.sign_x, sign_y, (at.side_x, flip_y), x, speed, q, first + k, k
                )
                for p, value in enumerate(merged):
                    put(level, value, p, q, k, at.half)
        return carry

    lax.fori_loop(0, CHEB, one_level, 0)
    fine = at.fine_y(False)
    between_own, between_got = between_y(at, at.sign_y, fine), between_y(at, -at.sign_y, fine)

    def two_level(p, carry):
        for k in range(count):
            mine = second_merge(at, level_own, (3, 5), between_own, (speed, speed_two), p, first + k, k)
            theirs = second_merge(at, level_got, (4, 6), between_got, (speed, speed_two), p, first + k, k)
            use(flipped(mine, theirs), p, k)
        return carry

    lax.fori_loop(0, CHEB, two_level, 0)


def piece_kernel(first, count, table, sides, speeds, own, got, send, keep, level, level_got):
    for half in range(2):
        at = Targets(half, table, sides, speeds)
        x, fine = at.x(False), at.fine_y(False)
        along_y = [fraction((at.sign_y * float(128.0 * z)) * fine) for z in POINTS]

        def to_send(values, p, k, half=half):
            for q, value in enumerate(values):
                put(send, value, p, q, k, half)

        def to_keep(values, p, k, at=at, x=x, along_y=along_y):
            along_x = fraction((at.sign_x * 128.0 * at.point(p)) * x)
            along_xz = fraction(along_x + float(64.0 * POINTS[first + k]) * at.z)
            for q, value in enumerate(values):
                cycles = (along_xz + along_y[q]) + at.speeds[2] * at.radius(7, p, q, first + k)
                cosine, sine = turn(cycles)
                place = (p, q, k, at.half)
                keep[(*place, 0)] = value[0] * cosine - value[1] * sine
                keep[(*place, 1)] = value[0] * sine + value[1] * cosine
                keep[(*place, 2)] = cosine
                keep[(*place, 3)] = sine

        @pl.when(sides[2] == 0)
        def _(at=at, to_send=to_send, to_keep=to_keep):
            parent(at, first, count, own, got, level)
            share_kind_0(at, first, count, True, level, to_send)
            share_kind_0(at, first, count, False, level, to_keep)

        @pl.when(sides[2] == 1)
        def _(at=at, to_send=to_send, to_keep=to_keep):
            share_kind_1(at, first, count, True, own, got, level, level_got, to_send)
            share_kind_1(at, first, count, False, own, got, level, level_got, to_keep)


def last_kernel(pieces, sides, *rest):
    out = rest[-1]
    side_x, side_y, kind = sides[0], sides[1], sides[2]

    def one(p, carry):
        for q in range(CHEB):
            point = (end(side_x, p), end(side_y, q))
            other = (end(kind, p), end(1 - kind, q))
            for place, (ref, k) in enumerate(pieces):
                keep, got = rest[2 * ref], rest[2 * ref + 1]
                for half in range(2):
                    re, im = got[(*other, k, half, 0)], got[(*other, k, half, 1)]
                    cosine, sine = keep[p, q, k, half, 2], keep[p, q, k, half, 3]
                    real = keep[p, q, k, half, 0] + (re * cosine - im * sine)
                    imaginary = keep[p, q, k, half, 1] + (re * sine + im * cosine)
                    row = 2 * ROWS * half
                    out[(*point, place, pl.ds(row, ROWS, stride=2), slice(None))] = real
                    out[(*point, place, pl.ds(row + 1, ROWS, stride=2), slice(None))] = imaginary
        return carry

    lax.fori_loop(0, CHEB, one, 0)


SMEM = pl.BlockSpec(memory_space=pltpu.SMEM)
VMEM = pl.BlockSpec(memory_space=pltpu.VMEM)
PARAMS = pltpu.CompilerParams(vmem_limit_bytes=VMEM_BYTES)


def pieces_of(count, parts):
    return (CHEB, CHEB, count, 2, parts, ROWS, LANES)


def cost(sets):
    return pl.CostEstimate(flops=sets * ROWS * LANES * 60, bytes_accessed=sets * 20000, transcendentals=0)


def run_piece(first, count, facts, own, got):
    return pl.pallas_call(
        functools.partial(piece_kernel, first, count),
        in_specs=[SMEM, SMEM, VMEM, VMEM, VMEM],
        out_specs=[VMEM, VMEM],
        out_shape=[jax.ShapeDtypeStruct(pieces_of(count, parts), jnp.float32) for parts in (2, 4)],
        scratch_shapes=[pltpu.VMEM(pieces_of(count, 2), jnp.float32)] * 2,
        compiler_params=PARAMS,
        cost_estimate=cost(450 * count),
        name=f"piece_{first}",
    )(*facts, own, got)


def run_last(group, facts, kept, arrived, out):
    pieces = [(ref, k) for ref, (_, count) in enumerate(PIECES[slice(*group)]) for k in range(count)]
    first, count = PIECES[group[0]][0], len(pieces)
    operands = [facts[1]]
    for piece in range(*group):
        operands += [kept[piece], arrived[piece]]
    in_specs = [SMEM] + [VMEM] * (len(operands) - 1)
    aliases = {}
    if out is not None:
        aliases = {len(operands): 0}
        in_specs.append(pl.BlockSpec(memory_space=pl.ANY))
        operands.append(out)
    return pl.pallas_call(
        functools.partial(last_kernel, pieces),
        grid=(1,),
        in_specs=in_specs,
        out_specs=pl.BlockSpec(
            (CHEB, CHEB, count, 4 * ROWS, LANES), lambda i: (0, 0, first // count, 0, 0)
        ),
        out_shape=jax.ShapeDtypeStruct((CHEB, CHEB, CHEB, 4 * ROWS, LANES), jnp.float32),
        input_output_aliases=aliases,
        compiler_params=PARAMS,
        cost_estimate=cost(25 * count),
        name=f"last_{first}",
    )(*operands)


def device_facts(speed_first, speed_second):
    width = [KMAX // lax.axis_size(axis) for axis in AXES]
    half_x, half_y = lax.axis_size("gx") // 2, lax.axis_size("gy") // 2
    index_x, index_y, index_z = (lax.axis_index(axis) for axis in AXES)
    side_x, side_y = index_x // half_x, index_y // half_y
    sign_x = 1.0 - 2.0 * side_x.astype(jnp.float32)
    sign_y = 1.0 - 2.0 * side_y.astype(jnp.float32)
    box_y = (2 * (index_y % half_y)).astype(jnp.float32) * width[1]
    center_x = ((2 * (index_x % half_x) + 1) * width[0]).astype(jnp.float32)
    center_z = (index_z.astype(jnp.float32) + 0.5) * width[2]
    own_y = box_y + (side_y.astype(jnp.float32) + 0.5) * width[1]
    far_y = box_y + (1.5 - side_y.astype(jnp.float32)) * width[1]
    middle_y = box_y + width[1]

    index = np.arange(LANES)
    inside = index < CHEB**3
    points = [
        np.where(inside, POINTS[index // step % CHEB], 0.0).astype(np.float32)
        for step in (CHEB * CHEB, CHEB, 1)
    ]
    child_x = sign_x * (width[0] * (points[0] - np.float32(0.5)))
    parent_x = sign_x * (2.0 * width[0] * points[0])
    child_y = sign_y * (width[1] * points[1])
    parent_y = sign_y * (2.0 * width[1] * points[1])
    pairs = (
        (child_x, own_y, child_y, own_y),
        (-child_x, own_y, child_y, own_y),
        (child_x, far_y, -child_y, far_y),
        (parent_x, own_y, child_y, own_y),
        (parent_x, far_y, -child_y, far_y),
        (parent_x, own_y, child_y, middle_y),
        (parent_x, far_y, -child_y, middle_y),
        (parent_x, middle_y, parent_y, middle_y),
    )
    grid_x = center_x + jnp.stack([pair[0] for pair in pairs])
    grid_y = jnp.stack([pair[1] + pair[2] for pair in pairs])
    center_y = jnp.stack([pair[3] for pair in pairs])[:, None]
    offset_z = (width[2] * points[2])[None]
    grid_z = center_z + offset_z
    numerator = (
        (grid_x - center_x) * (grid_x + center_x)
        + (grid_y - center_y) * (grid_y + center_y)
        + offset_z * (grid_z + center_z)
    )
    radius = jnp.sqrt(grid_x * grid_x + grid_y * grid_y + grid_z * grid_z) + jnp.sqrt(
        center_x * center_x + center_y * center_y + center_z * center_z
    )
    last = np.zeros((8, LANES), np.float32)
    last[0, :CHEB] = POINTS
    table = jnp.concatenate([numerator / radius, last], 0)
    kind = parity(kind_of(index_x, index_y, index_z, half_x, half_y))
    sides = jnp.stack([side_x, side_y, kind]).astype(jnp.int32)

    first = speed_first.reshape(TX, 2, TY * TZ)
    first_own = jnp.where(side_x == 0, first[:, 0], first[:, 1])
    first_far = jnp.where(side_x == 0, first[:, 1], first[:, 0])
    second = speed_second.reshape(TX, 2, TY, 2, TZ)
    second_own = jnp.where(side_x == 0, second[:, 0], second[:, 1])
    second_far = jnp.where(side_x == 0, second[:, 1], second[:, 0])
    speeds = [
        first_own,
        first_far,
        jnp.where(side_y == 0, second_own[:, :, 0], second_own[:, :, 1]),
        jnp.where(side_y == 0, second_own[:, :, 1], second_own[:, :, 0]),
        jnp.where(side_y == 0, second_far[:, :, 0], second_far[:, :, 1]),
    ]
    return table, sides, jnp.stack([speed.reshape(2 * ROWS, LANES) for speed in speeds])


def shards(source_coefs, speed_first, speed_second):
    weights = source_coefs.reshape(2, CHEB, CHEB, CHEB, 2 * ROWS, LANES)
    weights = weights.transpose(1, 2, 3, 4, 0, 5).reshape(CHEB, CHEB, CHEB, 4 * ROWS, LANES)
    raw = [weights[:, :, first : first + count] for first, count in PIECES]
    got = [exchange(piece, False) for piece in raw]
    facts = device_facts(speed_first, speed_second)
    sent, kept = [], []
    for k, (first, count) in enumerate(PIECES):
        send, keep = run_piece(first, count, facts, raw[k], got[k])
        sent.append(send)
        kept.append(keep)
    arrived = []
    for k, send in enumerate(sent):
        later = min(k + HOLD, len(sent) - 1)
        if later > k:
            send, sent[later] = lax.optimization_barrier((send, sent[later]))
        arrived.append(exchange(send, True))
    out = None
    for group in GROUPS:
        out = run_last(group, facts, kept, arrived, out)
    out = out.reshape(CHEB, CHEB, CHEB, 2 * ROWS, 2, LANES).transpose(4, 0, 1, 2, 3, 5)
    return out.reshape(source_coefs.shape)


def solution(mesh):
    in_specs = (P(None, None, None, None, ("gx", "gy", "gz")), P(), P())
    out_specs = P(None, None, None, None, ("gx", "gy", "gz"))
    return jax.shard_map(shards, mesh=mesh, in_specs=in_specs, out_specs=out_specs, check_vma=False)
```

```python
import functools

import jax
import jax.numpy as jnp
import numpy as np
from jax import lax
from jax.experimental import pallas as pl
from jax.experimental.pallas import tpu as pltpu
from jax.sharding import PartitionSpec as P

CHEB = 5
KMAX = 512
TX = 8
TY = 16
TZ = 16
ROWS = 8
LANES = 128
AXES = ("gx", "gy", "gz")
PIECES = ((0, 2), (2, 1), (3, 1), (4, 1))
HOLD = 0
GROUPS = ((0, 3), (3, 4))
VMEM_BYTES = 16 * 2**20
ROUNDER = 1.5 * 2.0**23
SINE = (4.442867903031852, -7.307443421308049, 3.594788078718595, -0.784374031470659)
COSINE = (
    1.41421349656502,
    -6.978850988239763,
    5.739461170697818,
    -1.8835629874053614,
    0.3106981920186687,
)

POINTS = 0.5 * np.cos(np.pi * np.arange(CHEB) / (CHEB - 1))
POINTS[CHEB // 2] = 0.0


def lagrange_table():
    shifted = (POINTS - 0.5) / 2.0
    table = np.ones((CHEB, CHEB))
    for target in range(CHEB):
        for factor in range(CHEB):
            if factor != target:
                table[target] *= (shifted - POINTS[factor]) / (POINTS[target] - POINTS[factor])
    return table


TABLE = lagrange_table()


def kind_of(index_x, index_y, index_z, half_x, half_y):
    return index_x % half_x ^ index_y % half_y ^ index_z


def parity(bits):
    return (bits ^ bits >> 1 ^ bits >> 2) & 1


def exchange(value, second):
    size_x, size_y, size_z = (lax.axis_size(axis) for axis in AXES)
    pairs = []
    for device in range(size_x * size_y * size_z):
        x, y, z = device // (size_y * size_z), device // size_z % size_y, device % size_z
        kind = parity(kind_of(x, y, z, size_x // 2, size_y // 2))
        if kind == int(second):
            x = (x + size_x // 2) % size_x
        else:
            y = (y + size_y // 2) % size_y
        pairs.append((device, (x * size_y + y) * size_z + z))
    return lax.ppermute(value, AXES, pairs)


def fraction(cycles):
    return cycles - ((cycles + ROUNDER) - ROUNDER)


def turn(cycles):
    part = fraction(cycles)
    square = part * part
    sine = SINE[-1] * square + SINE[-2]
    for factor in SINE[-3::-1]:
        sine = sine * square + factor
    sine = sine * part
    cosine = COSINE[-1] * square + COSINE[-2]
    for factor in COSINE[-3::-1]:
        cosine = cosine * square + factor
    return 1.0 - sine * sine, sine * cosine


def forward(value, cycles):
    cosine, sine = turn(cycles)
    return value[0] * cosine - value[1] * sine, value[0] * sine + value[1] * cosine


def backward(value, cycles):
    cosine, sine = turn(cycles)
    return value[0] * cosine + value[1] * sine, value[1] * cosine - value[0] * sine


def merge(values):
    merged = []
    for target in range(CHEB):
        parts = []
        for part in range(2):
            total = float(TABLE[target, 1]) * values[1][part]
            for point in (2, 3):
                total = total + float(TABLE[target, point]) * values[point][part]
            if target == 2:
                total = total + values[0][part]
            if target == 4:
                total = total + values[4][part]
            parts.append(total)
        merged.append(tuple(parts))
    return merged


def flipped(first, second):
    return [
        (a[0] + b[0], a[1] + b[1]) for a, b in zip(first, second[::-1], strict=True)
    ]


class Targets:
    def __init__(self, half, table, sides, speeds):
        row = lax.broadcasted_iota(jnp.int32, (ROWS, LANES), 0) + ROWS * half
        lane = lax.broadcasted_iota(jnp.int32, (ROWS, LANES), 1)
        self.along_x = lax.shift_right_logical(row, 1).astype(jnp.float32)
        self.along_y = (
            lax.bitwise_and(row, 1) * 8 + lax.shift_right_logical(lane, 4)
        ).astype(jnp.float32)
        self.along_z = lax.bitwise_and(lane, 15).astype(jnp.float32)
        self.z = (self.along_z + 0.5) / TZ
        self.y = (self.along_y + 0.5) / TY
        self.table = table
        self.half = half
        self.side_x, self.side_y = sides[0], sides[1]
        self.sign_x = 1.0 - 2.0 * self.side_x.astype(jnp.float32)
        self.sign_y = 1.0 - 2.0 * self.side_y.astype(jnp.float32)
        self.speeds = [speeds[k, ROWS * half : ROWS * (half + 1), :] for k in range(5)]

    def x(self, far):
        side = self.side_x.astype(jnp.float32)
        side = 1.0 - side if far else side
        return (2.0 * self.along_x + side + 0.5) / (2.0 * TX)

    def fine_y(self, far):
        side = self.side_y.astype(jnp.float32)
        side = 1.0 - side if far else side
        return (2.0 * self.along_y + side + 0.5) / (2.0 * TY)

    def point(self, index):
        return self.table[8, index]

    def radius(self, which, p, q, r):
        return self.table[which, p * (CHEB * CHEB) + q * CHEB + r]


def end(side, index):
    return index + side * (CHEB - 1 - 2 * index)


def first_merge(at, weights, which, sign_x, sign_y, flips, x, speed, q, r, r_local):
    flip_x, flip_y = flips
    rows = at.point(q) * (64.0 * sign_y) * at.y + at.point(r) * 64.0 * at.z
    rows = fraction(rows)
    turned = []
    for m in range(CHEB):
        cycles = (x[m] + rows) + speed * at.radius(which, m, q, r)
        point = (end(flip_x, m), end(flip_y, q), r_local)
        value = (
            weights[(*point, pl.ds(2 * ROWS * at.half, ROWS, stride=2), slice(None))],
            weights[(*point, pl.ds(2 * ROWS * at.half + 1, ROWS, stride=2), slice(None))],
        )
        turned.append(backward(value, cycles))
    return merge(turned)


def first_x(sign, x):
    return [fraction((sign * (64.0 * float(z - 0.5))) * x) for z in POINTS]


def between_y(at, sign, fine):
    return [
        fraction(sign * (float(64.0 * z) * at.y - float(64.0 * (z - 0.5)) * fine)) for z in POINTS
    ]


def second_merge(at, level, tables, between, speeds, p, r, r_local):
    turned = []
    for q in range(CHEB):
        cycles = (
            between[q]
            + speeds[0] * at.radius(tables[0], p, q, r)
            - speeds[1] * at.radius(tables[1], p, q, r)
        )
        value = (level[p, q, r_local, at.half, 0], level[p, q, r_local, at.half, 1])
        turned.append(forward(value, cycles))
    return merge(turned)


def put(ref, values, *place):
    ref[(*place, 0)] = values[0]
    ref[(*place, 1)] = values[1]


def parent(at, first, count, own, got, level):
    x = at.x(False)
    x_own, x_got = first_x(at.sign_x, x), first_x(-at.sign_x, x)

    def one(q, carry):
        for k in range(count):
            mine = first_merge(
                at, own, 0, at.sign_x, at.sign_y, (at.side_x, at.side_y), x_own, at.speeds[0], q, first + k, k
            )
            theirs = first_merge(
                at, got, 1, -at.sign_x, at.sign_y, (1 - at.side_x, at.side_y), x_got, at.speeds[0], q, first + k, k
            )
            for p, value in enumerate(flipped(mine, theirs)):
                put(level, value, p, q, k, at.half)
        return carry

    lax.fori_loop(0, CHEB, one, 0)


def share_kind_0(at, first, count, far, level, use):
    between = between_y(at, at.sign_y, at.fine_y(far))
    speeds = (at.speeds[0], at.speeds[3 if far else 2])

    def one(p, carry):
        for k in range(count):
            use(second_merge(at, level, (3, 5), between, speeds, p, first + k, k), p, k)
        return carry

    lax.fori_loop(0, CHEB, one, 0)


def share_kind_1(at, first, count, far, own, got, level_own, level_got, use):
    x = first_x(at.sign_x, at.x(far))
    speed, speed_two = at.speeds[int(far)], at.speeds[4 if far else 2]

    def one_level(q, carry):
        for k in range(count):
            for weights, which, sign_y, flip_y, level in (
                (own, 0, at.sign_y, at.side_y, level_own),
                (got, 2, -at.sign_y, 1 - at.side_y, level_got),
            ):
                merged = first_merge(
                    at, weights, which, at.sign_x, sign_y, (at.side_x, flip_y), x, speed, q, first + k, k
                )
                for p, value in enumerate(merged):
                    put(level, value, p, q, k, at.half)
        return carry

    lax.fori_loop(0, CHEB, one_level, 0)
    fine = at.fine_y(False)
    between_own, between_got = between_y(at, at.sign_y, fine), between_y(at, -at.sign_y, fine)

    def two_level(p, carry):
        for k in range(count):
            mine = second_merge(at, level_own, (3, 5), between_own, (speed, speed_two), p, first + k, k)
            theirs = second_merge(at, level_got, (4, 6), between_got, (speed, speed_two), p, first + k, k)
            use(flipped(mine, theirs), p, k)
        return carry

    lax.fori_loop(0, CHEB, two_level, 0)


def piece_kernel(first, count, table, sides, speeds, own, got, send, keep, level, level_got):
    for half in range(2):
        at = Targets(half, table, sides, speeds)
        x, fine = at.x(False), at.fine_y(False)
        along_y = [fraction((at.sign_y * float(128.0 * z)) * fine) for z in POINTS]

        def to_send(values, p, k, half=half):
            for q, value in enumerate(values):
                put(send, value, p, q, k, half)

        def to_keep(values, p, k, at=at, x=x, along_y=along_y):
            along_x = fraction((at.sign_x * 128.0 * at.point(p)) * x)
            along_xz = fraction(along_x + float(64.0 * POINTS[first + k]) * at.z)
            for q, value in enumerate(values):
                cycles = (along_xz + along_y[q]) + at.speeds[2] * at.radius(7, p, q, first + k)
                cosine, sine = turn(cycles)
                place = (p, q, k, at.half)
                keep[(*place, 0)] = value[0] * cosine - value[1] * sine
                keep[(*place, 1)] = value[0] * sine + value[1] * cosine
                keep[(*place, 2)] = cosine
                keep[(*place, 3)] = sine

        @pl.when(sides[2] == 0)
        def _(at=at, to_send=to_send, to_keep=to_keep):
            parent(at, first, count, own, got, level)
            share_kind_0(at, first, count, True, level, to_send)
            share_kind_0(at, first, count, False, level, to_keep)

        @pl.when(sides[2] == 1)
        def _(at=at, to_send=to_send, to_keep=to_keep):
            share_kind_1(at, first, count, True, own, got, level, level_got, to_send)
            share_kind_1(at, first, count, False, own, got, level, level_got, to_keep)


def last_kernel(pieces, *rest):
    out = rest[-1]
    half_x, half_y = lax.axis_size("gx") // 2, lax.axis_size("gy") // 2
    index_x, index_y, index_z = (lax.axis_index(axis) for axis in AXES)
    side_x, side_y = lax.div(index_x, half_x), lax.div(index_y, half_y)
    kind = parity(kind_of(index_x, index_y, index_z, half_x, half_y))

    def one(p, carry):
        for q in range(CHEB):
            point = (end(side_x, p), end(side_y, q))
            other = (end(kind, p), end(1 - kind, q))
            for place, (ref, k) in enumerate(pieces):
                keep, got = rest[2 * ref], rest[2 * ref + 1]
                for half in range(2):
                    re, im = got[(*other, k, half, 0)], got[(*other, k, half, 1)]
                    cosine, sine = keep[p, q, k, half, 2], keep[p, q, k, half, 3]
                    real = keep[p, q, k, half, 0] + (re * cosine - im * sine)
                    imaginary = keep[p, q, k, half, 1] + (re * sine + im * cosine)
                    row = 2 * ROWS * half
                    out[(*point, place, pl.ds(row, ROWS, stride=2), slice(None))] = real
                    out[(*point, place, pl.ds(row + 1, ROWS, stride=2), slice(None))] = imaginary
        return carry

    lax.fori_loop(0, CHEB, one, 0)


SMEM = pl.BlockSpec(memory_space=pltpu.SMEM)
VMEM = pl.BlockSpec(memory_space=pltpu.VMEM)
PARAMS = pltpu.CompilerParams(vmem_limit_bytes=VMEM_BYTES)


def pieces_of(count, parts):
    return (CHEB, CHEB, count, 2, parts, ROWS, LANES)


def cost(sets):
    return pl.CostEstimate(flops=sets * ROWS * LANES * 60, bytes_accessed=sets * 20000, transcendentals=0)


def run_piece(first, count, facts, own, got):
    return pl.pallas_call(
        functools.partial(piece_kernel, first, count),
        in_specs=[SMEM, SMEM, VMEM, VMEM, VMEM],
        out_specs=[VMEM, VMEM],
        out_shape=[jax.ShapeDtypeStruct(pieces_of(count, parts), jnp.float32) for parts in (2, 4)],
        scratch_shapes=[pltpu.VMEM(pieces_of(count, 2), jnp.float32)] * 2,
        compiler_params=PARAMS,
        cost_estimate=cost(450 * count),
        name=f"piece_{first}",
    )(*facts, own, got)


def run_last(group, kept, arrived, out):
    pieces = [(ref, k) for ref, (_, count) in enumerate(PIECES[slice(*group)]) for k in range(count)]
    first, count = PIECES[group[0]][0], len(pieces)
    operands = []
    for piece in range(*group):
        operands += [kept[piece], arrived[piece]]
    in_specs = [VMEM] * len(operands)
    aliases = {}
    if out is not None:
        aliases = {len(operands): 0}
        in_specs.append(pl.BlockSpec(memory_space=pl.ANY))
        operands.append(out)
    return pl.pallas_call(
        functools.partial(last_kernel, pieces),
        grid=(1,),
        in_specs=in_specs,
        out_specs=pl.BlockSpec(
            (CHEB, CHEB, count, 4 * ROWS, LANES), lambda i: (0, 0, first // count, 0, 0)
        ),
        out_shape=jax.ShapeDtypeStruct((CHEB, CHEB, CHEB, 4 * ROWS, LANES), jnp.float32),
        input_output_aliases=aliases,
        compiler_params=PARAMS,
        cost_estimate=cost(25 * count),
        name=f"last_{first}",
    )(*operands)


def device_facts(speed_first, speed_second):
    width = [KMAX // lax.axis_size(axis) for axis in AXES]
    half_x, half_y = lax.axis_size("gx") // 2, lax.axis_size("gy") // 2
    index_x, index_y, index_z = (lax.axis_index(axis) for axis in AXES)
    side_x, side_y = index_x // half_x, index_y // half_y
    sign_x = 1.0 - 2.0 * side_x.astype(jnp.float32)
    sign_y = 1.0 - 2.0 * side_y.astype(jnp.float32)
    box_y = (2 * (index_y % half_y)).astype(jnp.float32) * width[1]
    center_x = ((2 * (index_x % half_x) + 1) * width[0]).astype(jnp.float32)
    center_z = (index_z.astype(jnp.float32) + 0.5) * width[2]
    own_y = box_y + (side_y.astype(jnp.float32) + 0.5) * width[1]
    far_y = box_y + (1.5 - side_y.astype(jnp.float32)) * width[1]
    middle_y = box_y + width[1]

    index = np.arange(LANES)
    inside = index < CHEB**3
    points = [
        np.where(inside, POINTS[index // step % CHEB], 0.0).astype(np.float32)
        for step in (CHEB * CHEB, CHEB, 1)
    ]
    child_x = sign_x * (width[0] * (points[0] - np.float32(0.5)))
    parent_x = sign_x * (2.0 * width[0] * points[0])
    child_y = sign_y * (width[1] * points[1])
    parent_y = sign_y * (2.0 * width[1] * points[1])
    pairs = (
        (child_x, own_y, child_y, own_y),
        (-child_x, own_y, child_y, own_y),
        (child_x, far_y, -child_y, far_y),
        (parent_x, own_y, child_y, own_y),
        (parent_x, far_y, -child_y, far_y),
        (parent_x, own_y, child_y, middle_y),
        (parent_x, far_y, -child_y, middle_y),
        (parent_x, middle_y, parent_y, middle_y),
    )
    grid_x = center_x + jnp.stack([pair[0] for pair in pairs])
    grid_y = jnp.stack([pair[1] + pair[2] for pair in pairs])
    center_y = jnp.stack([pair[3] for pair in pairs])[:, None]
    offset_z = (width[2] * points[2])[None]
    grid_z = center_z + offset_z
    numerator = (
        (grid_x - center_x) * (grid_x + center_x)
        + (grid_y - center_y) * (grid_y + center_y)
        + offset_z * (grid_z + center_z)
    )
    radius = jnp.sqrt(grid_x * grid_x + grid_y * grid_y + grid_z * grid_z) + jnp.sqrt(
        center_x * center_x + center_y * center_y + center_z * center_z
    )
    last = np.zeros((8, LANES), np.float32)
    last[0, :CHEB] = POINTS
    table = jnp.concatenate([numerator / radius, last], 0)
    kind = parity(kind_of(index_x, index_y, index_z, half_x, half_y))
    sides = jnp.stack([side_x, side_y, kind]).astype(jnp.int32)

    first = speed_first.reshape(TX, 2, TY * TZ)
    first_own = jnp.where(side_x == 0, first[:, 0], first[:, 1])
    first_far = jnp.where(side_x == 0, first[:, 1], first[:, 0])
    second = speed_second.reshape(TX, 2, TY, 2, TZ)
    second_own = jnp.where(side_x == 0, second[:, 0], second[:, 1])
    second_far = jnp.where(side_x == 0, second[:, 1], second[:, 0])
    speeds = [
        first_own,
        first_far,
        jnp.where(side_y == 0, second_own[:, :, 0], second_own[:, :, 1]),
        jnp.where(side_y == 0, second_own[:, :, 1], second_own[:, :, 0]),
        jnp.where(side_y == 0, second_far[:, :, 0], second_far[:, :, 1]),
    ]
    return table, sides, jnp.stack([speed.reshape(2 * ROWS, LANES) for speed in speeds])


def shards(source_coefs, speed_first, speed_second):
    weights = source_coefs.reshape(2, CHEB, CHEB, CHEB, 2 * ROWS, LANES)
    weights = weights.transpose(1, 2, 3, 4, 0, 5).reshape(CHEB, CHEB, CHEB, 4 * ROWS, LANES)
    raw = [weights[:, :, first : first + count] for first, count in PIECES]
    got = [exchange(piece, False) for piece in raw]
    facts = device_facts(speed_first, speed_second)
    sent, kept = [], []
    for k, (first, count) in enumerate(PIECES):
        send, keep = run_piece(first, count, facts, raw[k], got[k])
        sent.append(send)
        kept.append(keep)
    arrived = []
    for k, send in enumerate(sent):
        later = min(k + HOLD, len(sent) - 1)
        if later > k:
            send, sent[later] = lax.optimization_barrier((send, sent[later]))
        arrived.append(exchange(send, True))
    out = None
    for group in GROUPS:
        out = run_last(group, kept, arrived, out)
    out = out.reshape(CHEB, CHEB, CHEB, 2 * ROWS, 2, LANES).transpose(4, 0, 1, 2, 3, 5)
    return out.reshape(source_coefs.shape)


def solution(mesh):
    in_specs = (P(None, None, None, None, ("gx", "gy", "gz")), P(), P())
    out_specs = P(None, None, None, None, ("gx", "gy", "gz"))
    return jax.shard_map(shards, mesh=mesh, in_specs=in_specs, out_specs=out_specs, check_vma=False)
```
